512 devices in a mesh: dp: 256 (over y, z, x), mp: 2 (over core).
Axes of the slice: x: 4, y: 8, z: 8, core: 2. Of those that a mesh axis runs over, the one named last changes fastest.
Arguments:
- acts: bfloat16 [65536, 1024], P('dp')
- grads_out: bfloat16 [65536, 2048], P('dp', 'mp')
- owners: int32 [2, 4], replicated, may hold values from 0 to 255, as said below
- left_stats: bfloat16 [256, 2, 512, 512], P('dp', 'mp')
- right_stats: bfloat16 [256, 2, 512, 512], P('dp', 'mp')
- left_root: bfloat16 [256, 2, 512, 512], P('dp', 'mp')
- right_root: bfloat16 [256, 2, 512, 512], P('dp', 'mp')
Outputs:
- update: bfloat16 [1024, 2048], P('dp', 'mp')
- left_new: bfloat16 [256, 2, 512, 512], P('dp', 'mp')
- right_new: bfloat16 [256, 2, 512, 512], P('dp', 'mp')
The draws below stay inside these ranges and needn't reach their ends.
Inputs may be any that keep to these rules, and one draw needn't show every extreme that they name: All 8 owners are different numbers; the smallest and the largest index of dp are always among them.
All inputs are finite; a program needn't handle non-finite values.
Results may differ from the reference program's by a relative error of at most 0.0065.
Values may be sent and summed in bfloat16 or wider, within the bound.
A program may use at most 64 MiB of HBM per device.

```python
import math
import jax
import jax.numpy as jnp
from jax import lax

B = 512
NBR = 2
NBC = 2
TOKENS = 65536
N_DP = 256
N_MP = 2


def symmetric_slots(key, diag_low, diag_high, spread, gain_low, gain_high):
    key_diag, key_off, key_gain = jax.random.split(key, 3)
    diagonal = jnp.exp(jax.random.uniform(key_diag, (N_DP, N_MP, B), jnp.float32, math.log(diag_low), math.log(diag_high)))
    slot_gain = jnp.exp(jax.random.uniform(key_gain, (N_DP, N_MP, 1, 1), jnp.float32, math.log(gain_low), math.log(gain_high)))
    noise = jax.random.normal(key_off, (N_DP, N_MP, B, B), jnp.float32)
    offdiag = (noise + jnp.swapaxes(noise, 2, 3)) * (spread * 0.7071)
    identity = jnp.eye(B, dtype=jnp.float32)
    matrix = offdiag * (1.0 - identity) + diagonal[..., None] * identity
    return (matrix * slot_gain).astype(jnp.bfloat16)


def draw_acts(key, part):
    key = jax.random.fold_in(key, 1)
    key_scale, key_base = jax.random.split(key, 2)
    columns = NBR * B
    col_scale = jnp.exp(jax.random.uniform(key_scale, (1, columns), jnp.float32, 0.0, math.log(10.0))) / 4.0
    base = jax.random.normal(key_base, (TOKENS, columns), jnp.float32)
    return (base * col_scale).astype(jnp.bfloat16)


def draw_grads_out(key, part):
    key = jax.random.fold_in(key, 2)
    key_scale, key_base = jax.random.split(key, 2)
    columns = N_MP * NBC * B
    position = jnp.arange(columns, dtype=jnp.float32)[None, :] / columns
    trend = jnp.exp(math.log(3.0) * position)
    col_scale = trend * jnp.exp(jax.random.uniform(key_scale, (1, columns), jnp.float32, 0.0, math.log(10.0))) / 6.0
    factor = 1.0 / jnp.sqrt(jnp.float32(TOKENS))
    base = jax.random.normal(key_base, (TOKENS, columns), jnp.float32)
    return (base * col_scale * factor).astype(jnp.bfloat16)


def draw_owners(key, part):
    key = jax.random.fold_in(key, 3)
    key_pick, key_order = jax.random.split(key)
    needed = N_MP * NBR * NBC
    middle = jax.random.permutation(key_pick, N_DP - 2).astype(jnp.int32) + 1
    chosen = jnp.concatenate([jnp.array([0, N_DP - 1], dtype=jnp.int32), middle[:needed - 2]])
    placed = jax.random.permutation(key_order, chosen)
    return placed.reshape(N_MP, NBR * NBC).astype(jnp.int32)


def draw_left_stats(key, part):
    key = jax.random.fold_in(key, 4)
    return symmetric_slots(key, 0.5, 2.0, 0.02, 1.0, 1.0)


def draw_right_stats(key, part):
    key = jax.random.fold_in(key, 5)
    return symmetric_slots(key, 0.5, 2.0, 0.02, 1.0, 1.0)


def draw_left_root(key, part):
    key = jax.random.fold_in(key, 6)
    return symmetric_slots(key, 0.5, 2.0, 0.02, 0.5, 2.0)


def draw_right_root(key, part):
    key = jax.random.fold_in(key, 8)
    return symmetric_slots(key, 0.5, 2.0, 0.02, 0.5, 2.0)


def setup_inputs(seed: int = 0) -> dict:
    key_list = jax.random.split(jax.random.key(seed), 8)
    return {
        "acts": draw_acts(jax.random.fold_in(key_list[7], 71), 0),
        "grads_out": draw_grads_out(jax.random.fold_in(key_list[7], 71), 0),
        "owners": draw_owners(jax.random.fold_in(key_list[7], 71), 0),
        "left_stats": draw_left_stats(jax.random.fold_in(key_list[7], 71), 0),
        "right_stats": draw_right_stats(jax.random.fold_in(key_list[7], 71), 0),
        "left_root": draw_left_root(jax.random.fold_in(key_list[7], 71), 0),
        "right_root": draw_right_root(jax.random.fold_in(key_list[7], 71), 0),
    }


stat_decay = 0.9
graft_eps = 1e-06

def reference(acts, grads_out, owners, left_stats, right_stats, left_root, right_root):
    gradient_sum = jnp.dot(acts.astype(jnp.float32).T, grads_out.astype(jnp.float32))
    gradient = gradient_sum.astype(jnp.bfloat16)
    left_new = left_stats
    right_new = right_stats
    columns = []
    for my_shard in range(N_MP):
        for block_col in range(NBC):
            row_parts = []
            for block_row in range(NBR):
                col_start = (my_shard * NBC + block_col) * B
                one_block = gradient[block_row * B:(block_row + 1) * B, col_start:col_start + B]
                owner_index = owners[my_shard, block_row * NBC + block_col]
                left_gram = lax.dot_general(one_block, one_block, (((1,), (1,)), ((), ())), preferred_element_type=jnp.float32)
                right_gram = lax.dot_general(one_block, one_block, (((0,), (0,)), ((), ())), preferred_element_type=jnp.float32)
                left_old = left_stats[owner_index, my_shard].astype(jnp.float32)
                right_old = right_stats[owner_index, my_shard].astype(jnp.float32)
                left_value = (stat_decay * left_old + (1.0 - stat_decay) * left_gram / B).astype(jnp.bfloat16)
                right_value = (stat_decay * right_old + (1.0 - stat_decay) * right_gram / B).astype(jnp.bfloat16)
                left_new = left_new.at[owner_index, my_shard].set(left_value)
                right_new = right_new.at[owner_index, my_shard].set(right_value)
                left_side = jnp.dot(left_root[owner_index, my_shard], one_block, preferred_element_type=jnp.float32).astype(jnp.bfloat16)
                product = jnp.dot(left_side, right_root[owner_index, my_shard], preferred_element_type=jnp.float32).astype(jnp.bfloat16)
                row_parts.append(product)
            columns.append(jnp.concatenate(row_parts, axis=0))
    preconditioned = jnp.concatenate(columns, axis=1)
    grad_square = jnp.sum(jnp.square(gradient.astype(jnp.float32)))
    precond_square = jnp.sum(jnp.square(preconditioned.astype(jnp.float32)))
    graft_scale = jnp.sqrt(grad_square / (precond_square + graft_eps))
    update = (graft_scale * preconditioned.astype(jnp.float32)).astype(jnp.bfloat16)
    return (update, left_new, right_new)
```

```python
import functools

import jax
import jax.numpy as jnp
from jax import lax
from jax.experimental import pallas as pl
from jax.experimental.pallas import tpu as pltpu
from jax.sharding import PartitionSpec as P

stat_decay = 0.9
graft_eps = 1e-06
MESH = pl.DeviceIdType.MESH
SIZE = {"y": 8, "z": 8, "x": 4}
SEND_ORDER = {8: (4, 3, 5, 2, 6, 1, 7), 4: (2, 1, 3)}
WAIT_ORDER = {8: (1, 7, 2, 6, 3, 5, 4), 4: (1, 3, 2)}
B = 512
F32 = jnp.float32
BF16 = jnp.bfloat16

SCRATCH = dict(
    a=((256, 1024), BF16),
    g=((256, 1024), BF16),
    left_old=((B, B), BF16),
    right_old=((B, B), BF16),
    left_root=((B, B), BF16),
    right_root=((B, B), BF16),
    sy=((8, 4, 64, 128), BF16),
    sz=((8, 4, 64, 128), BF16),
    sx=((4, 2, 4, 128, 128), BF16),
    ry=((8, 4, 64, 128), BF16),
    rz=((8, 4, 64, 128), BF16),
    rx=((4, 2, 4, 128, 128), BF16),
    m2z=((8, 96, 128), BF16),
    m2y=((8, 96, 128), BF16),
    r2z=((8, 96, 128), BF16),
    r2y=((8, 96, 128), BF16),
    m3x=((64, 128), BF16),
    m3y=((64, 128), BF16),
    m3z=((64, 128), BF16),
    r3x=((4, 64, 128), BF16),
    r3y=((8, 64, 128), BF16),
    r3z=((8, 64, 128), BF16),
    g4z=((8, 96, 128), BF16),
    g4y=((8, 96, 128), BF16),
    m5y=((8, 64, 128), BF16),
    m5z=((8, 64, 128), BF16),
    m5x=((4, 2, 128, 128), BF16),
    g5y=((8, 64, 128), BF16),
    g5z=((8, 64, 128), BF16),
    g5x=((4, 2, 128, 128), BF16),
    block=((B, B), BF16),
    perm1=((B, B), BF16),
    perm2=((B, B), BF16),
    ta=((8, 4, 16, 256), BF16),
    tbc=((4, 2, 128, 128), BF16),
    ua=((8, 4, 16, 256), BF16),
    ubc=((4, 2, 128, 128), BF16),
    va=((4, 4, 16, 256), BF16),
    vb=((8, 2, 32, 128), BF16),
    vc=((8, 4, 16, 128), BF16),
    wa=((4, 4, 16, 256), BF16),
    wb=((8, 2, 32, 128), BF16),
    wc=((8, 4, 16, 128), BF16),
    qy=((8, 8, 384), F32),
    qz=((8, 8, 128), F32),
    hy=((8, 8, 384), F32),
    hz=((8, 8, 128), F32),
    c0=((8, 128), F32),
    c1=((8, 128), F32),
    c2=((8, 128), F32),
    c3=((8, 128), F32),
    d0=((8, 128), F32),
    d1=((4, 8, 128), F32),
    d2=((8, 8, 128), F32),
    d3=((8, 8, 128), F32),
    left_out=((B, B), BF16),
    right_out=((B, B), BF16),
)
COPIES = 144


def dot(lhs, rhs, contract=((1,), (0,))):
    return lax.dot_general(lhs, rhs, (contract, ((), ())), preferred_element_type=F32)


def step_kernel(owners, acts, grads, left_stats, right_stats, left_roots, right_roots, update, left_new, right_new, *rest):
    s = dict(zip(SCRATCH, rest))
    send_sem, recv_sem, local_sem = rest[len(SCRATCH) :]
    me = lax.axis_index("dp")
    core = lax.axis_index("mp")
    at = {"y": me // 32, "z": (me // 4) % 8, "x": me % 4}
    my_y, my_z, my_x = at["y"], at["z"], at["x"]

    def index_of(y, z, x):
        return (y * 8 + z) * 4 + x

    def partner(axis, d):
        there = dict(at)
        there[axis] = (at[axis] + d) % SIZE[axis]
        return there[axis], index_of(**there)

    loads = []
    for k, (src, name) in enumerate(
        ((acts, "a"), (grads, "g"), (left_roots, "left_root"), (right_roots, "right_root"), (left_stats, "left_old"), (right_stats, "right_old"))
    ):
        loads.append(pltpu.make_async_copy(src, s[name], local_sem.at[k]))
        loads[-1].start()

    barrier = pltpu.get_barrier_semaphore()
    greeted = 0
    for axis in ("y", "z", "x"):
        for d in SEND_ORDER[SIZE[axis]]:
            pl.semaphore_signal(barrier, inc=1, device_id=(partner(axis, d)[1], core), device_id_type=MESH)
            greeted += 1
    pl.semaphore_signal(barrier, inc=1, device_id=(me, 1 - core), device_id_type=MESH)
    greeted += 1

    used = [0]
    started = []

    def send(src, dst, dp, mp):
        k = used[0]
        used[0] += 1
        copy = pltpu.make_async_remote_copy(
            src_ref=src, dst_ref=dst, send_sem=send_sem.at[k], recv_sem=recv_sem.at[k], device_id=(dp, mp), device_id_type=MESH
        )
        copy.start()
        started.append(copy)
        return copy

    def exchange(axis, src, dst):
        copies = {}
        for d in SEND_ORDER[SIZE[axis]]:
            t, dp = partner(axis, d)
            copies[d] = send(src(t, d), dst(d), dp, core)
        return [copies[d] for d in WAIT_ORDER[SIZE[axis]]]

    def arrive(copies):
        for copy in copies:
            copy.wait_recv()

    def total(own, received, n, *index):
        value = own.astype(F32)
        for d in range(1, n):
            value = value + received[(d, *index)].astype(F32)
        return value

    loads[0].wait()
    loads[1].wait()
    g_value = s["g"][...]
    for i in range(4):
        for r in range(2):
            lhs = s["a"][:, r * B + i * 128 : r * B + (i + 1) * 128]
            value = dot(lhs, g_value, ((0,), (0,))).astype(BF16)
            for c in range(2):
                b = 2 * r + c
                piece = value[:, c * B : (c + 1) * B]
                s["sy"][2 * i, b] = piece[:64, :128]
                s["sy"][2 * i + 1, b] = piece[64:, :128]
                s["sz"][2 * i, b] = piece[:64, 128:256]
                s["sz"][2 * i + 1, b] = piece[64:, 128:256]
                s["sx"][i, 0, b] = piece[:, 256:384]
                s["sx"][i, 1, b] = piece[:, 384:]

    pl.semaphore_wait(barrier, greeted)
    copies_x = exchange("x", lambda t, d: s["sx"].at[t], lambda d: s["rx"].at[d])
    copies_y = exchange("y", lambda t, d: s["sy"].at[t], lambda d: s["ry"].at[d])
    copies_z = exchange("z", lambda t, d: s["sz"].at[t], lambda d: s["rz"].at[d])

    loads[2].wait()
    row = lax.broadcasted_iota(jnp.int32, (B, B), 0)
    col = lax.broadcasted_iota(jnp.int32, (B, B), 1)
    x_part, k_part = row // 128, row % 4
    source1 = ((row // 4) % 4) * 128 + ((row // 16) % 8) * 16 + x_part * 4 + k_part
    source2 = ((row // 32) % 4) * 128 + ((row // 4) % 8) * 16 + x_part * 4 + k_part
    for source, name in ((source1, "perm1"), (source2, "perm2")):
        pick = jnp.where(col == source, 1.0, 0.0).astype(BF16)
        s[name][...] = dot(pick, s["left_root"][...]).astype(BF16)

    arrive(copies_x)
    for t in range(8):
        b, half = t // 2, (t % 2) * 64
        for which, name in ((0, "m2y"), (1, "m2z")):
            index = (which, b, slice(half, half + 64))
            s[name][t, 32:96] = total(s["sx"][(my_x, *index)], s["rx"], 4, *index).astype(BF16)

    def narrow_sums(own, received, name, place):
        for t in range(8):
            index = (t // 2, slice((t % 2) * 32, (t % 2) * 32 + 32))
            s[name][t, 0:32] = total(own[(place, *index)], received, 8, *index).astype(BF16)

    arrive(copies_y)
    narrow_sums(s["sy"], s["ry"], "m2z", my_y)
    copies_z2 = exchange("z", lambda t, d: s["m2z"].at[t], lambda d: s["r2z"].at[d])
    arrive(copies_z)
    narrow_sums(s["sz"], s["rz"], "m2y", my_z)
    copies_y2 = exchange("y", lambda t, d: s["m2y"].at[t], lambda d: s["r2y"].at[d])

    arrive(copies_z2)
    value = total(s["m2z"][my_z], s["r2z"], 8).astype(BF16)
    s["m3x"][0:32] = value[:32]
    s["m3y"][...] = value[32:]
    copies_y3 = exchange("y", lambda t, d: s["m3y"], lambda d: s["r3y"].at[d])
    arrive(copies_y2)
    value = total(s["m2y"][my_y], s["r2y"], 8).astype(BF16)
    s["m3x"][32:64] = value[:32]
    s["m3z"][...] = value[32:]
    copies_z3 = exchange("z", lambda t, d: s["m3z"], lambda d: s["r3z"].at[d])
    copies_x3 = exchange("x", lambda t, d: s["m3x"], lambda d: s["r3x"].at[d])

    arrive(copies_x3)
    value = total(s["m3x"][...], s["r3x"], 4).astype(BF16)
    s["g4z"][my_z, 0:32] = value[:32]
    s["g4y"][my_y, 0:32] = value[32:]
    arrive(copies_y3)
    s["g4z"][my_z, 32:96] = total(s["m3y"][...], s["r3y"], 8).astype(BF16)
    copies_z4 = exchange("z", lambda t, d: s["g4z"].at[my_z], lambda d: s["g4z"].at[my_z])
    arrive(copies_z3)
    s["g4y"][my_y, 32:96] = total(s["m3z"][...], s["r3z"], 8).astype(BF16)
    copies_y4 = exchange("y", lambda t, d: s["g4y"].at[my_y], lambda d: s["g4y"].at[my_y])

    owner = [owners[core, b] for b in range(4)]
    owner_y = [o // 32 for o in owner]
    owner_z = [(o // 4) % 8 for o in owner]
    owner_x = [o % 4 for o in owner]

    def block_of(dp):
        b = jnp.int32(0)
        for k in range(1, 4):
            b = jnp.where(owner[k] == dp, k, b)
        return b

    my_block = block_of(me)
    is_owner = (owner[0] == me) | (my_block > 0)

    arrive(copies_z4)

    def narrow_part(source, b):
        return jnp.concatenate([s[source][2 * b, 0:32], s[source][2 * b + 1, 0:32]], axis=0)

    def wide_part(source, b):
        return jnp.concatenate([s[source][2 * b, 32:96], s[source][2 * b + 1, 32:96]], axis=0)

    for d in range(1, 8):
        s["m5y"][d] = narrow_part("g4z", block_of(partner("y", d)[1]))
    copies_y5 = exchange("y", lambda t, d: s["m5y"].at[d], lambda d: s["g5y"].at[my_y])
    s["g5y"][my_y] = narrow_part("g4z", my_block)
    for d in range(1, 4):
        s["m5x"][d, 1] = wide_part("g4z", block_of(partner("x", d)[1]))
    s["g5x"][my_x, 1] = wide_part("g4z", my_block)
    arrive(copies_y4)
    for d in range(1, 4):
        s["m5x"][d, 0] = wide_part("g4y", block_of(partner("x", d)[1]))
    copies_x5 = exchange("x", lambda t, d: s["m5x"].at[d], lambda d: s["g5x"].at[my_x])
    for d in range(1, 8):
        s["m5z"][d] = narrow_part("g4y", block_of(partner("z", d)[1]))
    copies_z5 = exchange("z", lambda t, d: s["m5z"].at[d], lambda d: s["g5z"].at[my_z])
    s["g5x"][my_x, 0] = wide_part("g4y", my_block)
    s["g5z"][my_z] = narrow_part("g4y", my_block)

    arrive(copies_y5)
    for k in range(8):
        s["block"][k * 64 : (k + 1) * 64, 0:128] = s["g5y"][k]
    arrive(copies_x5)
    for k in range(4):
        s["block"][k * 128 : (k + 1) * 128, 256:384] = s["g5x"][k, 0]
        s["block"][k * 128 : (k + 1) * 128, 384:512] = s["g5x"][k, 1]
    arrive(copies_z5)
    for k in range(8):
        s["block"][k * 64 : (k + 1) * 64, 128:256] = s["g5z"][k]

    one_block = s["block"][...]
    loads[3].wait()
    left1 = dot(s["perm1"][...], one_block).astype(BF16)
    part_a = dot(left1, s["right_root"][:, 0:256]).astype(BF16)
    for k in range(4):
        for z in range(8):
            row0 = (k * 8 + z) * 16
            s["ta"][z, k] = part_a[row0 : row0 + 16]
    copies_ta = exchange("z", lambda t, d: s["ta"].at[t], lambda d: s["ua"].at[my_z])
    s["ua"][my_z] = s["ta"][my_z]
    left2 = dot(s["perm2"][...], one_block).astype(BF16)
    part_b = dot(left2, s["right_root"][:, 256:384]).astype(BF16)
    part_c = dot(left1, s["right_root"][:, 384:512]).astype(BF16)
    for k in range(4):
        s["tbc"][k, 0] = part_b[k * 128 : (k + 1) * 128]
        s["tbc"][k, 1] = part_c[k * 128 : (k + 1) * 128]
    copies_tbc = exchange("x", lambda t, d: s["tbc"].at[t], lambda d: s["ubc"].at[my_x])
    s["ubc"][my_x] = s["tbc"][my_x]

    def square_sum(value):
        value = value.astype(F32)
        return jnp.sum(jnp.sum(value * value, axis=0, keepdims=True), axis=1, keepdims=True)

    grad_square = square_sum(one_block)
    precond_square = square_sum(part_a) + square_sum(part_b) + square_sum(part_c)
    lane = lax.broadcasted_iota(jnp.int32, (8, 128), 1)
    both = jnp.where(lane == 0, grad_square, precond_square)
    s["c0"][...] = jnp.where(is_owner, both, jnp.zeros_like(both))
    copy_c0 = send(s["c0"], s["d0"], me, 1 - core)

    def new_stat(old, gram):
        old = old.astype(F32)
        return jnp.where(is_owner, stat_decay * old + (1.0 - stat_decay) * gram / B, old).astype(BF16)

    copy_c0.wait_recv()
    s["c1"][...] = s["c0"][...] + s["d0"][...]
    copies_c1 = exchange("x", lambda t, d: s["c1"], lambda d: s["d1"].at[d])

    arrive(copies_tbc)
    for t in range(8):
        for c in range(2):
            b = 2 * (t // 4) + c
            s["vb"][t, c] = s["ubc"][owner_x[b], 0, (t % 4) * 32 : (t % 4) * 32 + 32]
        for b in range(4):
            s["vc"][t, b] = s["ubc"][owner_x[b], 1, t * 16 : (t + 1) * 16]
    copies_vb = exchange("y", lambda t, d: s["vb"].at[t], lambda d: s["wb"].at[my_y])
    copies_vc = exchange("z", lambda t, d: s["vc"].at[t], lambda d: s["wc"].at[my_z])
    s["wb"][my_y] = s["vb"][my_y]
    s["wc"][my_z] = s["vc"][my_z]
    arrive(copies_c1)
    s["c2"][...] = total(s["c1"][...], s["d1"], 4)
    copies_c2 = exchange("y", lambda t, d: s["c2"], lambda d: s["d2"].at[d])
    arrive(copies_ta)
    for t in range(4):
        for b in range(4):
            s["va"][t, b] = s["ua"][owner_z[b], t]
    copies_va = exchange("x", lambda t, d: s["va"].at[t], lambda d: s["wa"].at[my_x])
    s["wa"][my_x] = s["va"][my_x]
    arrive(copies_c2)
    s["c3"][...] = total(s["c2"][...], s["d2"], 8)
    copies_c3 = exchange("z", lambda t, d: s["c3"], lambda d: s["d3"].at[d])

    loads[4].wait()
    s["left_out"][...] = new_stat(s["left_old"][...], dot(one_block, one_block, ((1,), (1,))))
    stores = [pltpu.make_async_copy(s["left_out"], left_new, local_sem.at[6])]
    stores[0].start()

    my_half = my_y // 4
    arrive(copies_vb)
    from_y, from_z = [], []
    for c in range(2):
        o = owners[core, 2 * my_half + c]
        from_y.append(o // 32)
        from_z.append((o // 4) % 8)
    for c in range(2):
        value = s["wb"][from_y[c], c].astype(F32)
        for t in range(8):
            s["qz"][t, 4 * c : 4 * c + 4] = value[4 * t : 4 * t + 4]
    copies_qz = exchange("z", lambda t, d: s["qz"].at[t], lambda d: s["hz"].at[my_z])
    s["hz"][my_z] = s["qz"][my_z]
    arrive(copies_vc)
    arrive(copies_va)
    for b in range(4):
        r, c = b // 2, b % 2
        value_a = s["wa"][owner_x[b], b].astype(F32)
        value_c = s["wc"][owner_z[b], b].astype(F32)
        for k in range(4):
            s["qy"][4 * r + k, 4 * c : 4 * c + 4, 0:256] = value_a[4 * k : 4 * k + 4]
            s["qy"][4 * r + k, 4 * c : 4 * c + 4, 256:384] = value_c[4 * k : 4 * k + 4]
    copies_qy = exchange("y", lambda t, d: s["qy"].at[t], lambda d: s["hy"].at[my_y])
    s["hy"][my_y] = s["qy"][my_y]

    loads[5].wait()
    s["right_out"][...] = new_stat(s["right_old"][...], dot(one_block, one_block, ((0,), (0,))))
    stores.append(pltpu.make_async_copy(s["right_out"], right_new, local_sem.at[7]))
    stores[1].start()

    arrive(copies_c3)
    sums = total(s["c3"][...], s["d3"], 8)
    scale = jnp.sqrt(sums[0:1, 0:1] / (sums[0:1, 1:2] + graft_eps))
    arrive(copies_qz)
    arrive(copies_qy)
    for c in range(2):
        value = s["hy"][from_y[c]][4 * c : 4 * c + 4]
        update[:, c * B : c * B + 256] = value[:, 0:256] * scale
        update[:, c * B + 384 : (c + 1) * B] = value[:, 256:384] * scale
        update[:, c * B + 256 : c * B + 384] = s["hz"][from_z[c]][4 * c : 4 * c + 4] * scale

    for copy in started:
        copy.wait_send()
    for copy in stores:
        copy.wait()


def shards(acts, grads_out, owners, left_stats, right_stats, left_root, right_root):
    anywhere = pl.BlockSpec(memory_space=pl.ANY)
    stat = jax.ShapeDtypeStruct((B, B), BF16)
    update, left_new, right_new = pl.pallas_call(
        step_kernel,
        out_shape=(jax.ShapeDtypeStruct((4, 1024), F32), stat, stat),
        in_specs=[pl.BlockSpec(memory_space=pltpu.SMEM)] + [anywhere] * 6,
        out_specs=(pl.BlockSpec(memory_space=pltpu.VMEM), anywhere, anywhere),
        scratch_shapes=[pltpu.VMEM(shape, dtype) for shape, dtype in SCRATCH.values()]
        + [
            pltpu.SemaphoreType.DMA((COPIES,)),
            pltpu.SemaphoreType.DMA((COPIES,)),
            pltpu.SemaphoreType.DMA((8,)),
        ],
        compiler_params=pltpu.CompilerParams(collective_id=0, has_side_effects=True, vmem_limit_bytes=40 * 2**20),
        name="shampoo_step",
    )(owners, acts, grads_out, left_stats[0, 0], right_stats[0, 0], left_root[0, 0], right_root[0, 0])
    return (update.astype(BF16), left_new.reshape(left_stats.shape), right_new.reshape(right_stats.shape))


def solution(mesh):
    return jax.shard_map(
        shards,
        mesh=mesh,
        in_specs=(
            P("dp", None),
            P("dp", "mp"),
            P(),
            P("dp", "mp", None, None),
            P("dp", "mp", None, None),
            P("dp", "mp", None, None),
            P("dp", "mp", None, None),
        ),
        out_specs=(P("dp", "mp"), P("dp", "mp", None, None), P("dp", "mp", None, None)),
        check_vma=False,
    )
```

```python
import functools

import jax
import jax.numpy as jnp
from jax import lax
from jax.experimental import pallas as pl
from jax.experimental.pallas import tpu as pltpu
from jax.sharding import PartitionSpec as P

stat_decay = 0.9
graft_eps = 1e-06
MESH = pl.DeviceIdType.MESH
SIZE = {"y": 8, "z": 8, "x": 4}
SEND_ORDER = {8: (4, 3, 5, 2, 6, 1, 7), 4: (2, 1, 3)}
B = 512
F32 = jnp.float32
BF16 = jnp.bfloat16

SCRATCH = dict(
    a=((256, 1024), BF16),
    at=((1024, 256), BF16),
    g=((256, 1024), BF16),
    left_old=((B, B), BF16),
    right_old=((B, B), BF16),
    left_root=((B, B), BF16),
    right_root=((B, B), BF16),
    sy=((8, 4, 64, 128), BF16),
    sz=((8, 4, 64, 128), BF16),
    sx=((4, 2, 4, 128, 128), BF16),
    ry=((8, 4, 64, 128), BF16),
    rz=((8, 4, 64, 128), BF16),
    rx=((4, 2, 4, 128, 128), BF16),
    m2z=((8, 96, 128), BF16),
    m2y=((8, 96, 128), BF16),
    r2z=((8, 96, 128), BF16),
    r2y=((8, 96, 128), BF16),
    m3x=((64, 128), BF16),
    m3y=((64, 128), BF16),
    m3z=((64, 128), BF16),
    r3x=((4, 64, 128), BF16),
    r3y=((8, 64, 128), BF16),
    r3z=((8, 64, 128), BF16),
    g4z=((8, 96, 128), BF16),
    g4y=((8, 96, 128), BF16),
    m5y=((8, 64, 128), BF16),
    m5z=((8, 64, 128), BF16),
    m5x=((4, 2, 128, 128), BF16),
    g5y=((8, 64, 128), BF16),
    g5z=((8, 64, 128), BF16),
    g5x=((4, 2, 128, 128), BF16),
    block=((B, B), BF16),
    perm1=((B, B), BF16),
    perm2=((B, B), BF16),
    ta=((8, 4, 16, 256), BF16),
    tbc=((4, 2, 128, 128), BF16),
    ua=((8, 4, 16, 256), BF16),
    ubc=((4, 2, 128, 128), BF16),
    va=((4, 4, 16, 256), BF16),
    vb=((8, 2, 32, 128), BF16),
    vc=((8, 4, 16, 128), BF16),
    wa=((4, 4, 16, 256), BF16),
    wb=((8, 2, 32, 128), BF16),
    wc=((8, 4, 16, 128), BF16),
    qy=((8, 8, 384), F32),
    qz=((8, 8, 128), F32),
    hy=((8, 8, 384), F32),
    hz=((8, 8, 128), F32),
    c0=((8, 128), F32),
    c1=((8, 128), F32),
    c2=((8, 128), F32),
    c3=((8, 128), F32),
    d0=((8, 128), F32),
    d1=((4, 8, 128), F32),
    d2=((8, 8, 128), F32),
    d3=((8, 8, 128), F32),
    left_out=((B, B), BF16),
    right_out=((B, B), BF16),
)
EXCHANGES = 28


def dot(lhs, rhs, contract=((1,), (0,))):
    return lax.dot_general(lhs, rhs, (contract, ((), ())), preferred_element_type=F32)


def step_kernel(owners_in, acts, grads, left_stats, right_stats, left_roots, right_roots, update, left_new, right_new, *rest):
    s = dict(zip(SCRATCH, rest))
    send_sem, recv_sem, local_sem = rest[len(SCRATCH) : len(SCRATCH) + 3]
    me = lax.axis_index("dp")
    core = lax.axis_index("mp")
    at = {"y": me // 32, "z": (me // 4) % 8, "x": me % 4}
    my_y, my_z, my_x = at["y"], at["z"], at["x"]

    def index_of(y, z, x):
        return (y * 8 + z) * 4 + x

    def partner(axis, d):
        there = dict(at)
        there[axis] = (at[axis] + d) % SIZE[axis]
        return there[axis], index_of(**there)

    loads = []
    for k, (src, name) in enumerate(
        ((acts, "a"), (grads, "g"), (left_roots, "left_root"), (right_roots, "right_root"), (left_stats, "left_old"), (right_stats, "right_old"))
    ):
        loads.append(pltpu.make_async_copy(src, s[name], local_sem.at[k]))
    for k, (src, name) in enumerate(((acts, "a"), (grads, "g"))):
        for part in range(4):
            rows = pl.ds(part * 64, 64)
            pltpu.make_async_copy(src.at[rows], s[name].at[rows], local_sem.at[k]).start()

    owners = rest[len(SCRATCH) + 3]
    load_owners = pltpu.make_async_copy(owners_in, owners, local_sem.at[8])
    load_owners.start()

    barrier = pltpu.get_barrier_semaphore()
    greeted = 0
    for axis in ("y", "z", "x"):
        for d in SEND_ORDER[SIZE[axis]]:
            pl.semaphore_signal(barrier, inc=1, device_id=(partner(axis, d)[1], core), device_id_type=MESH)
            greeted += 1
    pl.semaphore_signal(barrier, inc=1, device_id=(me, 1 - core), device_id_type=MESH)
    greeted += 1

    used = [0]
    started = []

    def remote(src, dst, k, dp, mp):
        return pltpu.make_async_remote_copy(
            src_ref=src, dst_ref=dst, send_sem=send_sem.at[k], recv_sem=recv_sem.at[k], device_id=(dp, mp), device_id_type=MESH
        )

    def exchange(axis, src, into, dst=None):
        k = used[0]
        used[0] += 1
        n = SIZE[axis]
        for d in SEND_ORDER[n]:
            t, dp = partner(axis, d)
            remote(src(t, d), dst(d) if dst else s[into].at[d], k, dp, core).start()
        slots = s[into].at[0 : n - 1]
        started.append(remote(slots, slots, k, partner(axis, 1)[1], core))
        return started[-1]

    def to_sibling(src, dst):
        k = used[0]
        used[0] += 1
        copy = remote(src, dst, k, me, 1 - core)
        copy.start()
        started.append(copy)
        return copy

    def arrive(copy):
        copy.wait_recv()

    def total(own, received, n, *index):
        value = own.astype(F32)
        for d in range(1, n):
            value = value + received[(d, *index)].astype(F32)
        return value

    loads[0].wait()
    loads[1].wait()
    for k in range(4):
        s["at"][k * 256 : (k + 1) * 256] = s["a"][:, k * 256 : (k + 1) * 256].T

    def products(lane):
        for r in range(2):
            for c in range(2):
                rhs = s["g"][:, c * B + lane : c * B + lane + 256]
                yield 2 * r + c, dot(s["at"][r * B : (r + 1) * B], rhs).astype(BF16)

    for b, value in products(0):
        for t in range(8):
            s["sy"][t, b] = value[t * 64 : (t + 1) * 64, :128]
            s["sz"][t, b] = value[t * 64 : (t + 1) * 64, 128:]
    pl.semaphore_wait(barrier, greeted)
    copies_y = exchange("y", lambda t, d: s["sy"].at[t], "ry")
    copies_z = exchange("z", lambda t, d: s["sz"].at[t], "rz")
    for b, value in products(256):
        for t in range(4):
            s["sx"][t, 0, b] = value[t * 128 : (t + 1) * 128, :128]
            s["sx"][t, 1, b] = value[t * 128 : (t + 1) * 128, 128:]
    copies_x = exchange("x", lambda t, d: s["sx"].at[t], "rx")
    for load in loads[2:]:
        load.start()

    row = lax.broadcasted_iota(jnp.int32, (B, B), 0)
    col = lax.broadcasted_iota(jnp.int32, (B, B), 1)
    x_part, k_part = row // 128, row % 4
    source1 = ((row // 4) % 4) * 128 + ((row // 16) % 8) * 16 + x_part * 4 + k_part
    source2 = ((row // 32) % 4) * 128 + ((row // 4) % 8) * 16 + x_part * 4 + k_part
    loads[2].wait()
    for source, name in ((source1, "perm1"), (source2, "perm2")):
        pick = jnp.where(col == source, 1.0, 0.0).astype(BF16)
        s[name][...] = dot(pick, s["left_root"][...]).astype(BF16)

    arrive(copies_x)
    for t in range(8):
        b, half = t // 2, (t % 2) * 64
        for which, name in ((0, "m2y"), (1, "m2z")):
            index = (which, b, slice(half, half + 64))
            s[name][t, 32:96] = total(s["sx"][(my_x, *index)], s["rx"], 4, *index).astype(BF16)

    def narrow_sums(own, received, name, place):
        for t in range(8):
            index = (t // 2, slice((t % 2) * 32, (t % 2) * 32 + 32))
            s[name][t, 0:32] = total(own[(place, *index)], received, 8, *index).astype(BF16)

    arrive(copies_y)
    narrow_sums(s["sy"], s["ry"], "m2z", my_y)
    copies_z2 = exchange("z", lambda t, d: s["m2z"].at[t], "r2z")
    arrive(copies_z)
    narrow_sums(s["sz"], s["rz"], "m2y", my_z)
    copies_y2 = exchange("y", lambda t, d: s["m2y"].at[t], "r2y")

    arrive(copies_z2)
    value = total(s["m2z"][my_z], s["r2z"], 8).astype(BF16)
    s["m3x"][0:32] = value[:32]
    s["m3y"][...] = value[32:]
    copies_y3 = exchange("y", lambda t, d: s["m3y"], "r3y")
    arrive(copies_y2)
    value = total(s["m2y"][my_y], s["r2y"], 8).astype(BF16)
    s["m3x"][32:64] = value[:32]
    s["m3z"][...] = value[32:]
    copies_z3 = exchange("z", lambda t, d: s["m3z"], "r3z")
    copies_x3 = exchange("x", lambda t, d: s["m3x"], "r3x")

    arrive(copies_x3)
    value = total(s["m3x"][...], s["r3x"], 4).astype(BF16)
    s["g4z"][my_z, 0:32] = value[:32]
    s["g4y"][my_y, 0:32] = value[32:]
    arrive(copies_y3)
    s["g4z"][my_z, 32:96] = total(s["m3y"][...], s["r3y"], 8).astype(BF16)
    copies_z4 = exchange("z", lambda t, d: s["g4z"].at[my_z], "g4z", lambda d: s["g4z"].at[my_z])
    arrive(copies_z3)
    s["g4y"][my_y, 32:96] = total(s["m3z"][...], s["r3z"], 8).astype(BF16)
    copies_y4 = exchange("y", lambda t, d: s["g4y"].at[my_y], "g4y", lambda d: s["g4y"].at[my_y])

    load_owners.wait()
    owner = [owners[core, b] for b in range(4)]
    owner_y = [o // 32 for o in owner]
    owner_z = [(o // 4) % 8 for o in owner]
    owner_x = [o % 4 for o in owner]

    def block_of(dp):
        b = jnp.int32(0)
        for k in range(1, 4):
            b = jnp.where(owner[k] == dp, k, b)
        return b

    my_block = block_of(me)
    is_owner = (owner[0] == me) | (my_block > 0)

    arrive(copies_z4)

    def narrow_part(source, b):
        return jnp.concatenate([s[source][2 * b, 0:32], s[source][2 * b + 1, 0:32]], axis=0)

    def wide_part(source, b):
        return jnp.concatenate([s[source][2 * b, 32:96], s[source][2 * b + 1, 32:96]], axis=0)

    for d in range(1, 8):
        s["m5y"][d] = narrow_part("g4z", block_of(partner("y", d)[1]))
    copies_y5 = exchange("y", lambda t, d: s["m5y"].at[d], "g5y", lambda d: s["g5y"].at[my_y])
    s["g5y"][my_y] = narrow_part("g4z", my_block)
    for d in range(1, 4):
        s["m5x"][d, 1] = wide_part("g4z", block_of(partner("x", d)[1]))
    s["g5x"][my_x, 1] = wide_part("g4z", my_block)
    arrive(copies_y4)
    for d in range(1, 4):
        s["m5x"][d, 0] = wide_part("g4y", block_of(partner("x", d)[1]))
    copies_x5 = exchange("x", lambda t, d: s["m5x"].at[d], "g5x", lambda d: s["g5x"].at[my_x])
    for d in range(1, 8):
        s["m5z"][d] = narrow_part("g4y", block_of(partner("z", d)[1]))
    copies_z5 = exchange("z", lambda t, d: s["m5z"].at[d], "g5z", lambda d: s["g5z"].at[my_z])
    s["g5x"][my_x, 0] = wide_part("g4y", my_block)
    s["g5z"][my_z] = narrow_part("g4y", my_block)

    arrive(copies_y5)
    for k in range(8):
        s["block"][k * 64 : (k + 1) * 64, 0:128] = s["g5y"][k]
    arrive(copies_x5)
    for k in range(4):
        s["block"][k * 128 : (k + 1) * 128, 256:384] = s["g5x"][k, 0]
        s["block"][k * 128 : (k + 1) * 128, 384:512] = s["g5x"][k, 1]
    arrive(copies_z5)
    for k in range(8):
        s["block"][k * 64 : (k + 1) * 64, 128:256] = s["g5z"][k]

    one_block = s["block"][...]
    loads[3].wait()
    left1 = dot(s["perm1"][...], one_block).astype(BF16)
    part_a = dot(left1, s["right_root"][:, 0:256]).astype(BF16)
    for k in range(4):
        for z in range(8):
            row0 = (k * 8 + z) * 16
            s["ta"][z, k] = part_a[row0 : row0 + 16]
    copies_ta = exchange("z", lambda t, d: s["ta"].at[t], "ua", lambda d: s["ua"].at[my_z])
    s["ua"][my_z] = s["ta"][my_z]
    left2 = dot(s["perm2"][...], one_block).astype(BF16)
    part_b = dot(left2, s["right_root"][:, 256:384]).astype(BF16)
    part_c = dot(left1, s["right_root"][:, 384:512]).astype(BF16)
    for k in range(4):
        s["tbc"][k, 0] = part_b[k * 128 : (k + 1) * 128]
        s["tbc"][k, 1] = part_c[k * 128 : (k + 1) * 128]
    copies_tbc = exchange("x", lambda t, d: s["tbc"].at[t], "ubc", lambda d: s["ubc"].at[my_x])
    s["ubc"][my_x] = s["tbc"][my_x]

    def square_sum(value):
        value = value.astype(F32)
        return jnp.sum(jnp.sum(value * value, axis=0, keepdims=True), axis=1, keepdims=True)

    grad_square = square_sum(one_block)
    precond_square = square_sum(part_a) + square_sum(part_b) + square_sum(part_c)
    lane = lax.broadcasted_iota(jnp.int32, (8, 128), 1)
    both = jnp.where(lane == 0, grad_square, precond_square)
    s["c0"][...] = jnp.where(is_owner, both, jnp.zeros_like(both))
    copy_c0 = to_sibling(s["c0"], s["d0"])

    def new_stat(old, gram):
        old = old.astype(F32)
        return jnp.where(is_owner, stat_decay * old + (1.0 - stat_decay) * gram / B, old).astype(BF16)

    arrive(copy_c0)
    s["c1"][...] = s["c0"][...] + s["d0"][...]
    copies_c1 = exchange("x", lambda t, d: s["c1"], "d1")

    arrive(copies_tbc)
    for t in range(8):
        for c in range(2):
            b = 2 * (t // 4) + c
            s["vb"][t, c] = s["ubc"][owner_x[b], 0, (t % 4) * 32 : (t % 4) * 32 + 32]
        for b in range(4):
            s["vc"][t, b] = s["ubc"][owner_x[b], 1, t * 16 : (t + 1) * 16]
    copies_vb = exchange("y", lambda t, d: s["vb"].at[t], "wb", lambda d: s["wb"].at[my_y])
    copies_vc = exchange("z", lambda t, d: s["vc"].at[t], "wc", lambda d: s["wc"].at[my_z])
    s["wb"][my_y] = s["vb"][my_y]
    s["wc"][my_z] = s["vc"][my_z]
    arrive(copies_c1)
    s["c2"][...] = total(s["c1"][...], s["d1"], 4)
    copies_c2 = exchange("y", lambda t, d: s["c2"], "d2")
    arrive(copies_ta)
    for t in range(4):
        for b in range(4):
            s["va"][t, b] = s["ua"][owner_z[b], t]
    copies_va = exchange("x", lambda t, d: s["va"].at[t], "wa", lambda d: s["wa"].at[my_x])
    s["wa"][my_x] = s["va"][my_x]
    arrive(copies_c2)
    s["c3"][...] = total(s["c2"][...], s["d2"], 8)
    copies_c3 = exchange("z", lambda t, d: s["c3"], "d3")

    loads[4].wait()
    s["left_out"][...] = new_stat(s["left_old"][...], dot(one_block, one_block, ((1,), (1,))))
    stores = [pltpu.make_async_copy(s["left_out"], left_new, local_sem.at[6])]
    stores[0].start()

    my_half = my_y // 4
    arrive(copies_vb)
    from_y, from_z = [], []
    for c in range(2):
        o = owners[core, 2 * my_half + c]
        from_y.append(o // 32)
        from_z.append((o // 4) % 8)
    for c in range(2):
        value = s["wb"][from_y[c], c].astype(F32)
        for t in range(8):
            s["qz"][t, 4 * c : 4 * c + 4] = value[4 * t : 4 * t + 4]
    copies_qz = exchange("z", lambda t, d: s["qz"].at[t], "hz", lambda d: s["hz"].at[my_z])
    s["hz"][my_z] = s["qz"][my_z]
    arrive(copies_vc)
    arrive(copies_va)
    for b in range(4):
        r, c = b // 2, b % 2
        value_a = s["wa"][owner_x[b], b].astype(F32)
        value_c = s["wc"][owner_z[b], b].astype(F32)
        for k in range(4):
            s["qy"][4 * r + k, 4 * c : 4 * c + 4, 0:256] = value_a[4 * k : 4 * k + 4]
            s["qy"][4 * r + k, 4 * c : 4 * c + 4, 256:384] = value_c[4 * k : 4 * k + 4]
    copies_qy = exchange("y", lambda t, d: s["qy"].at[t], "hy", lambda d: s["hy"].at[my_y])
    s["hy"][my_y] = s["qy"][my_y]

    loads[5].wait()
    s["right_out"][...] = new_stat(s["right_old"][...], dot(one_block, one_block, ((0,), (0,))))
    stores.append(pltpu.make_async_copy(s["right_out"], right_new, local_sem.at[7]))
    stores[1].start()

    arrive(copies_c3)
    sums = total(s["c3"][...], s["d3"], 8)
    scale = jnp.sqrt(sums[0:1, 0:1] / (sums[0:1, 1:2] + graft_eps))
    arrive(copies_qz)
    arrive(copies_qy)
    for c in range(2):
        value = s["hy"][from_y[c]][4 * c : 4 * c + 4]
        update[:, c * B : c * B + 256] = value[:, 0:256] * scale
        update[:, c * B + 384 : (c + 1) * B] = value[:, 256:384] * scale
        update[:, c * B + 256 : c * B + 384] = s["hz"][from_z[c]][4 * c : 4 * c + 4] * scale

    for copy in started:
        copy.wait_send()
    for copy in stores:
        copy.wait()


def shards(acts, grads_out, owners, left_stats, right_stats, left_root, right_root):
    anywhere = pl.BlockSpec(memory_space=pl.ANY)
    stat = jax.ShapeDtypeStruct((B, B), BF16)
    update, left_new, right_new = pl.pallas_call(
        step_kernel,
        out_shape=(jax.ShapeDtypeStruct((4, 1024), F32), stat, stat),
        in_specs=[anywhere] * 7,
        out_specs=(pl.BlockSpec(memory_space=pltpu.VMEM), anywhere, anywhere),
        scratch_shapes=[pltpu.VMEM(shape, dtype) for shape, dtype in SCRATCH.values()]
        + [
            pltpu.SemaphoreType.DMA((EXCHANGES,)),
            pltpu.SemaphoreType.DMA((EXCHANGES,)),
            pltpu.SemaphoreType.DMA((9,)),
            pltpu.SMEM((2, 4), jnp.int32),
        ],
        compiler_params=pltpu.CompilerParams(collective_id=0, has_side_effects=True, vmem_limit_bytes=int(52.5 * 2**20)),
        name="shampoo_step",
    )(owners, acts, grads_out, left_stats[0, 0], right_stats[0, 0], left_root[0, 0], right_root[0, 0])
    return (update.astype(BF16), left_new.reshape(left_stats.shape), right_new.reshape(right_stats.shape))


def solution(mesh):
    return jax.shard_map(
        shards,
        mesh=mesh,
        in_specs=(
            P("dp", None),
            P("dp", "mp"),
            P(),
            P("dp", "mp", None, None),
            P("dp", "mp", None, None),
            P("dp", "mp", None, None),
            P("dp", "mp", None, None),
        ),
        out_specs=(P("dp", "mp"), P("dp", "mp", None, None), P("dp", "mp", None, None)),
        check_vma=False,
    )
```

```python
import functools

import jax
import jax.numpy as jnp
from jax import lax
from jax.experimental import pallas as pl
from jax.experimental.pallas import tpu as pltpu
from jax.sharding import PartitionSpec as P

stat_decay = 0.9
graft_eps = 1e-06
MESH = pl.DeviceIdType.MESH
SIZE = {"y": 8, "z": 8, "x": 4}
SEND_ORDER = {8: (4, 3, 5, 2, 6, 1, 7), 4: (2, 1, 3)}
B = 512
F32 = jnp.float32
BF16 = jnp.bfloat16

SCRATCH = dict(
    a=((256, 1024), BF16),
    at=((1024, 256), BF16),
    g=((256, 1024), BF16),
    left_old=((B, B), BF16),
    right_old=((B, B), BF16),
    left_root=((B, B), BF16),
    right_root=((B, B), BF16),
    sy=((8, 4, 64, 128), BF16),
    sz=((8, 4, 64, 128), BF16),
    sx=((4, 2, 4, 128, 128), BF16),
    fy=((2, 4, 64, 128), BF16),
    fz=((2, 4, 64, 128), BF16),
    fx=((2, 4, 128, 128), BF16),
    ey=((2, 2, 64, 128), BF16),
    ez=((2, 2, 64, 128), BF16),
    qy1=((2, 4, 64, 128), BF16),
    qz1=((2, 4, 64, 128), BF16),
    qx1=((2, 4, 128, 128), BF16),
    ry=((4, 4, 64, 128), BF16),
    rz=((4, 4, 64, 128), BF16),
    rx=((2, 2, 4, 128, 128), BF16),
    m2z=((8, 96, 128), BF16),
    m2y=((8, 96, 128), BF16),
    r2z=((8, 96, 128), BF16),
    r2y=((8, 96, 128), BF16),
    m3x=((64, 128), BF16),
    m3y=((64, 128), BF16),
    m3z=((64, 128), BF16),
    r3x=((4, 64, 128), BF16),
    r3y=((8, 64, 128), BF16),
    r3z=((8, 64, 128), BF16),
    g4z=((8, 96, 128), BF16),
    g4y=((8, 96, 128), BF16),
    m5y=((8, 64, 128), BF16),
    m5z=((8, 64, 128), BF16),
    m5x=((4, 2, 128, 128), BF16),
    g5y=((8, 64, 128), BF16),
    g5z=((8, 64, 128), BF16),
    g5x=((4, 2, 128, 128), BF16),
    block=((B, B), BF16),
    perm1=((B, B), BF16),
    perm2=((B, B), BF16),
    ta=((8, 4, 16, 256), BF16),
    tbc=((4, 2, 128, 128), BF16),
    ua=((8, 4, 16, 256), BF16),
    ubc=((4, 2, 128, 128), BF16),
    va=((4, 4, 16, 256), BF16),
    vb=((8, 2, 32, 128), BF16),
    vc=((8, 4, 16, 128), BF16),
    wa=((4, 4, 16, 256), BF16),
    wb=((8, 2, 32, 128), BF16),
    wc=((8, 4, 16, 128), BF16),
    qy=((8, 8, 384), F32),
    qz=((8, 8, 128), F32),
    hy=((8, 8, 384), F32),
    hz=((8, 8, 128), F32),
    c0=((8, 128), F32),
    c1=((8, 128), F32),
    c2=((8, 128), F32),
    c3=((8, 128), F32),
    d0=((8, 128), F32),
    d1=((4, 8, 128), F32),
    d2=((8, 8, 128), F32),
    d3=((8, 8, 128), F32),
    left_out=((B, B), BF16),
    right_out=((B, B), BF16),
)
EXCHANGES = 46


def dot(lhs, rhs, contract=((1,), (0,))):
    return lax.dot_general(lhs, rhs, (contract, ((), ())), preferred_element_type=F32)


def step_kernel(owners_in, acts, grads, left_stats, right_stats, left_roots, right_roots, update, left_new, right_new, *rest):
    s = dict(zip(SCRATCH, rest))
    send_sem, recv_sem, local_sem = rest[len(SCRATCH) : len(SCRATCH) + 3]
    me = lax.axis_index("dp")
    core = lax.axis_index("mp")
    at = {"y": me // 32, "z": (me // 4) % 8, "x": me % 4}
    my_y, my_z, my_x = at["y"], at["z"], at["x"]

    def index_of(y, z, x):
        return (y * 8 + z) * 4 + x

    def partner(axis, d):
        there = dict(at)
        there[axis] = (at[axis] + d) % SIZE[axis]
        return there[axis], index_of(**there)

    loads = []
    for k, (src, name) in enumerate(
        ((acts, "a"), (grads, "g"), (left_roots, "left_root"), (right_roots, "right_root"), (left_stats, "left_old"), (right_stats, "right_old"))
    ):
        loads.append(pltpu.make_async_copy(src, s[name], local_sem.at[k]))
    for k, (src, name) in enumerate(((acts, "a"), (grads, "g"))):
        for part in range(4):
            rows = pl.ds(part * 64, 64)
            pltpu.make_async_copy(src.at[rows], s[name].at[rows], local_sem.at[k]).start()

    owners = rest[len(SCRATCH) + 3]
    load_owners = pltpu.make_async_copy(owners_in, owners, local_sem.at[8])
    load_owners.start()

    barrier = pltpu.get_barrier_semaphore()
    greeted = 0
    for axis in ("y", "z", "x"):
        for d in SEND_ORDER[SIZE[axis]]:
            pl.semaphore_signal(barrier, inc=1, device_id=(partner(axis, d)[1], core), device_id_type=MESH)
            greeted += 1
    pl.semaphore_signal(barrier, inc=1, device_id=(me, 1 - core), device_id_type=MESH)
    greeted += 1

    used = [0]
    started = []

    def remote(src, dst, k, dp, mp):
        return pltpu.make_async_remote_copy(
            src_ref=src, dst_ref=dst, send_sem=send_sem.at[k], recv_sem=recv_sem.at[k], device_id=(dp, mp), device_id_type=MESH
        )

    def exchange(axis, src, into, dst=None):
        k = used[0]
        used[0] += 1
        n = SIZE[axis]
        for d in SEND_ORDER[n]:
            t, dp = partner(axis, d)
            remote(src(t, d), dst(d) if dst else s[into].at[d], k, dp, core).start()
        slots = s[into].at[0 : n - 1]
        started.append(remote(slots, slots, k, partner(axis, 1)[1], core))
        return started[-1]

    def send(src, dst, dp, mp):
        k = used[0]
        used[0] += 1
        copy = remote(src, dst, k, dp, mp)
        copy.start()
        started.append(copy)
        return copy

    def arrive(*copies):
        for copy in copies:
            copy.wait_recv()

    def total(own, received, n, *index):
        value = own.astype(F32)
        for d in n:
            value = value + received[(d, *index)].astype(F32)
        return value

    loads[0].wait()
    loads[1].wait()
    for k in range(4):
        s["at"][k * 256 : (k + 1) * 256] = s["a"][:, k * 256 : (k + 1) * 256].T

    def products(lane):
        for r in range(2):
            for c in range(2):
                rhs = s["g"][:, c * B + lane : c * B + lane + 256]
                yield 2 * r + c, dot(s["at"][r * B : (r + 1) * B], rhs).astype(BF16)

    for b, value in products(0):
        for t in range(8):
            s["sy"][t, b] = value[t * 64 : (t + 1) * 64, :128]
            s["sz"][t, b] = value[t * 64 : (t + 1) * 64, 128:]
    pl.semaphore_wait(barrier, greeted)
    def away(axis, d):
        t, dp = partner(axis, d % SIZE[axis])
        return t, dp

    def first_sends(axis, own, full, half):
        t4 = away(axis, 4)[0]
        h0 = send(s[own].at[t4, 0:2], s[half].at[0], away(axis, 2)[1], core)
        h1 = send(s[own].at[t4, 2:4], s[half].at[1], away(axis, -2)[1], core)
        f0 = send(s[own].at[away(axis, 3)[0]], s[full].at[0], away(axis, 1)[1], core)
        f1 = send(s[own].at[away(axis, -3)[0]], s[full].at[1], away(axis, -1)[1], core)
        return [f0, f1, h0, h1]

    def neighbour_sends(axis, own, received):
        return [send(s[own].at[away(axis, d)[0]], s[received].at[k], away(axis, d)[1], core) for k, d in enumerate((1, -1))]

    relay_y = first_sends("y", "sy", "fy", "ey")
    relay_z = first_sends("z", "sz", "fz", "ez")
    copies_y = neighbour_sends("y", "sy", "ry")
    copies_z = neighbour_sends("z", "sz", "rz")

    for b, value in products(256):
        for t in range(4):
            s["sx"][t, 0, b] = value[t * 128 : (t + 1) * 128, :128]
            s["sx"][t, 1, b] = value[t * 128 : (t + 1) * 128, 128:]
    relay_x = [send(s["sx"].at[away("x", 2)[0], k], s["fx"].at[k], away("x", d)[1], core) for k, d in enumerate((1, -1))]
    copies_x = [send(s["sx"].at[away("x", d)[0], 1 - k], s["rx"].at[k, 1 - k], away("x", d)[1], core) for k, d in enumerate((1, -1))]

    for load in loads[2:]:
        load.start()

    def merge(axis, own, full, half, merged, received):
        copies = []
        for k, d in enumerate((2, -2)):
            t, dp = away(axis, d)
            for b in range(4):
                value = s[own][t, b].astype(F32) + s[full][k, b].astype(F32)
                if b // 2 == k:
                    value = value + s[half][k, b % 2].astype(F32)
                s[merged][k, b] = value.astype(BF16)
            copies.append(send(s[merged].at[k], s[received].at[2 + k], dp, core))
        return copies

    arrive(*relay_y)
    copies_y += merge("y", "sy", "fy", "ey", "qy1", "ry")
    arrive(*relay_z)
    copies_z += merge("z", "sz", "fz", "ez", "qz1", "rz")
    arrive(*relay_x)
    for k, d in enumerate((1, -1)):
        t, dp = away("x", d)
        for b in range(4):
            s["qx1"][k, b] = (s["sx"][t, k, b].astype(F32) + s["fx"][k, b].astype(F32)).astype(BF16)
        copies_x.append(send(s["qx1"].at[k], s["rx"].at[k, k], dp, core))

    arrive(*copies_x)
    for t in range(8):
        b, half = t // 2, (t % 2) * 64
        for which, name in ((0, "m2y"), (1, "m2z")):
            index = (which, b, slice(half, half + 64))
            s[name][t, 32:96] = total(s["sx"][(my_x, *index)], s["rx"], range(2), *index).astype(BF16)

    def narrow_sums(own, received, name, place):
        for t in range(8):
            index = (t // 2, slice((t % 2) * 32, (t % 2) * 32 + 32))
            s[name][t, 0:32] = total(own[(place, *index)], received, range(4), *index).astype(BF16)

    arrive(*copies_y)
    narrow_sums(s["sy"], s["ry"], "m2z", my_y)
    copies_z2 = exchange("z", lambda t, d: s["m2z"].at[t], "r2z")
    arrive(*copies_z)
    narrow_sums(s["sz"], s["rz"], "m2y", my_z)
    copies_y2 = exchange("y", lambda t, d: s["m2y"].at[t], "r2y")

    row = lax.broadcasted_iota(jnp.int32, (B, B), 0)
    col = lax.broadcasted_iota(jnp.int32, (B, B), 1)
    x_part, k_part = row // 128, row % 4
    source1 = ((row // 4) % 4) * 128 + ((row // 16) % 8) * 16 + x_part * 4 + k_part
    source2 = ((row // 32) % 4) * 128 + ((row // 4) % 8) * 16 + x_part * 4 + k_part
    loads[2].wait()
    for source, name in ((source1, "perm1"), (source2, "perm2")):
        pick = jnp.where(col == source, 1.0, 0.0).astype(BF16)
        s[name][...] = dot(pick, s["left_root"][...]).astype(BF16)

    arrive(copies_z2)
    value = total(s["m2z"][my_z], s["r2z"], range(1, 8)).astype(BF16)
    s["m3x"][0:32] = value[:32]
    s["m3y"][...] = value[32:]
    copies_y3 = exchange("y", lambda t, d: s["m3y"], "r3y")
    arrive(copies_y2)
    value = total(s["m2y"][my_y], s["r2y"], range(1, 8)).astype(BF16)
    s["m3x"][32:64] = value[:32]
    s["m3z"][...] = value[32:]
    copies_z3 = exchange("z", lambda t, d: s["m3z"], "r3z")
    copies_x3 = exchange("x", lambda t, d: s["m3x"], "r3x")

    arrive(copies_x3)
    value = total(s["m3x"][...], s["r3x"], range(1, 4)).astype(BF16)
    s["g4z"][my_z, 0:32] = value[:32]
    s["g4y"][my_y, 0:32] = value[32:]
    arrive(copies_y3)
    s["g4z"][my_z, 32:96] = total(s["m3y"][...], s["r3y"], range(1, 8)).astype(BF16)
    copies_z4 = exchange("z", lambda t, d: s["g4z"].at[my_z], "g4z", lambda d: s["g4z"].at[my_z])
    arrive(copies_z3)
    s["g4y"][my_y, 32:96] = total(s["m3z"][...], s["r3z"], range(1, 8)).astype(BF16)
    copies_y4 = exchange("y", lambda t, d: s["g4y"].at[my_y], "g4y", lambda d: s["g4y"].at[my_y])

    load_owners.wait()
    owner = [owners[core, b] for b in range(4)]
    owner_y = [o // 32 for o in owner]
    owner_z = [(o // 4) % 8 for o in owner]
    owner_x = [o % 4 for o in owner]

    def block_of(dp):
        b = jnp.int32(0)
        for k in range(1, 4):
            b = jnp.where(owner[k] == dp, k, b)
        return b

    my_block = block_of(me)
    is_owner = (owner[0] == me) | (my_block > 0)

    arrive(copies_z4)

    def narrow_part(source, b):
        return jnp.concatenate([s[source][2 * b, 0:32], s[source][2 * b + 1, 0:32]], axis=0)

    def wide_part(source, b):
        return jnp.concatenate([s[source][2 * b, 32:96], s[source][2 * b + 1, 32:96]], axis=0)

    for d in range(1, 8):
        s["m5y"][d] = narrow_part("g4z", block_of(partner("y", d)[1]))
    copies_y5 = exchange("y", lambda t, d: s["m5y"].at[d], "g5y", lambda d: s["g5y"].at[my_y])
    s["g5y"][my_y] = narrow_part("g4z", my_block)
    for d in range(1, 4):
        s["m5x"][d, 1] = wide_part("g4z", block_of(partner("x", d)[1]))
    s["g5x"][my_x, 1] = wide_part("g4z", my_block)
    arrive(copies_y4)
    for d in range(1, 4):
        s["m5x"][d, 0] = wide_part("g4y", block_of(partner("x", d)[1]))
    copies_x5 = exchange("x", lambda t, d: s["m5x"].at[d], "g5x", lambda d: s["g5x"].at[my_x])
    for d in range(1, 8):
        s["m5z"][d] = narrow_part("g4y", block_of(partner("z", d)[1]))
    copies_z5 = exchange("z", lambda t, d: s["m5z"].at[d], "g5z", lambda d: s["g5z"].at[my_z])
    s["g5x"][my_x, 0] = wide_part("g4y", my_block)
    s["g5z"][my_z] = narrow_part("g4y", my_block)

    arrive(copies_y5)
    for k in range(8):
        s["block"][k * 64 : (k + 1) * 64, 0:128] = s["g5y"][k]
    arrive(copies_x5)
    for k in range(4):
        s["block"][k * 128 : (k + 1) * 128, 256:384] = s["g5x"][k, 0]
        s["block"][k * 128 : (k + 1) * 128, 384:512] = s["g5x"][k, 1]
    arrive(copies_z5)
    for k in range(8):
        s["block"][k * 64 : (k + 1) * 64, 128:256] = s["g5z"][k]

    one_block = s["block"][...]
    loads[3].wait()
    left1 = dot(s["perm1"][...], one_block).astype(BF16)
    part_a = dot(left1, s["right_root"][:, 0:256]).astype(BF16)
    for k in range(4):
        for z in range(8):
            row0 = (k * 8 + z) * 16
            s["ta"][z, k] = part_a[row0 : row0 + 16]
    copies_ta = exchange("z", lambda t, d: s["ta"].at[t], "ua", lambda d: s["ua"].at[my_z])
    s["ua"][my_z] = s["ta"][my_z]
    left2 = dot(s["perm2"][...], one_block).astype(BF16)
    part_b = dot(left2, s["right_root"][:, 256:384]).astype(BF16)
    part_c = dot(left1, s["right_root"][:, 384:512]).astype(BF16)
    for k in range(4):
        s["tbc"][k, 0] = part_b[k * 128 : (k + 1) * 128]
        s["tbc"][k, 1] = part_c[k * 128 : (k + 1) * 128]
    copies_tbc = exchange("x", lambda t, d: s["tbc"].at[t], "ubc", lambda d: s["ubc"].at[my_x])
    s["ubc"][my_x] = s["tbc"][my_x]

    def square_sum(value):
        value = value.astype(F32)
        return jnp.sum(jnp.sum(value * value, axis=0, keepdims=True), axis=1, keepdims=True)

    grad_square = square_sum(one_block)
    precond_square = square_sum(part_a) + square_sum(part_b) + square_sum(part_c)
    lane = lax.broadcasted_iota(jnp.int32, (8, 128), 1)
    both = jnp.where(lane == 0, grad_square, precond_square)
    s["c0"][...] = jnp.where(is_owner, both, jnp.zeros_like(both))
    copy_c0 = send(s["c0"], s["d0"], me, 1 - core)

    def new_stat(old, gram):
        old = old.astype(F32)
        return jnp.where(is_owner, stat_decay * old + (1.0 - stat_decay) * gram / B, old).astype(BF16)

    arrive(copy_c0)
    s["c1"][...] = s["c0"][...] + s["d0"][...]
    copies_c1 = exchange("x", lambda t, d: s["c1"], "d1")

    early = len(started) - 4
    for copy in started[:early]:
        copy.wait_send()

    arrive(copies_tbc)
    arrive(copies_c1)
    s["c2"][...] = total(s["c1"][...], s["d1"], range(1, 4))
    copies_c2 = exchange("y", lambda t, d: s["c2"], "d2")
    for t in range(8):
        for c in range(2):
            b = 2 * (t // 4) + c
            s["vb"][t, c] = s["ubc"][owner_x[b], 0, (t % 4) * 32 : (t % 4) * 32 + 32]
        for b in range(4):
            s["vc"][t, b] = s["ubc"][owner_x[b], 1, t * 16 : (t + 1) * 16]
    copies_vb = exchange("y", lambda t, d: s["vb"].at[t], "wb", lambda d: s["wb"].at[my_y])
    copies_vc = exchange("z", lambda t, d: s["vc"].at[t], "wc", lambda d: s["wc"].at[my_z])
    s["wb"][my_y] = s["vb"][my_y]
    s["wc"][my_z] = s["vc"][my_z]
    arrive(copies_ta)
    for t in range(4):
        for b in range(4):
            s["va"][t, b] = s["ua"][owner_z[b], t]
    copies_va = exchange("x", lambda t, d: s["va"].at[t], "wa", lambda d: s["wa"].at[my_x])
    s["wa"][my_x] = s["va"][my_x]
    arrive(copies_c2)
    s["c3"][...] = total(s["c2"][...], s["d2"], range(1, 8))
    copies_c3 = exchange("z", lambda t, d: s["c3"], "d3")

    loads[4].wait()
    s["left_out"][...] = new_stat(s["left_old"][...], dot(one_block, one_block, ((1,), (1,))))
    stores = [pltpu.make_async_copy(s["left_out"], left_new, local_sem.at[6])]
    stores[0].start()

    my_half = my_y // 4
    arrive(copies_vb)
    from_y, from_z = [], []
    for c in range(2):
        o = owners[core, 2 * my_half + c]
        from_y.append(o // 32)
        from_z.append((o // 4) % 8)
    for c in range(2):
        value = s["wb"][from_y[c], c].astype(F32)
        for t in range(8):
            s["qz"][t, 4 * c : 4 * c + 4] = value[4 * t : 4 * t + 4]
    copies_qz = exchange("z", lambda t, d: s["qz"].at[t], "hz", lambda d: s["hz"].at[my_z])
    s["hz"][my_z] = s["qz"][my_z]
    arrive(copies_vc)
    arrive(copies_va)
    for b in range(4):
        r, c = b // 2, b % 2
        value_a = s["wa"][owner_x[b], b].astype(F32)
        value_c = s["wc"][owner_z[b], b].astype(F32)
        for k in range(4):
            s["qy"][4 * r + k, 4 * c : 4 * c + 4, 0:256] = value_a[4 * k : 4 * k + 4]
            s["qy"][4 * r + k, 4 * c : 4 * c + 4, 256:384] = value_c[4 * k : 4 * k + 4]
    copies_qy = exchange("y", lambda t, d: s["qy"].at[t], "hy", lambda d: s["hy"].at[my_y])
    s["hy"][my_y] = s["qy"][my_y]

    loads[5].wait()
    s["right_out"][...] = new_stat(s["right_old"][...], dot(one_block, one_block, ((0,), (0,))))
    stores.append(pltpu.make_async_copy(s["right_out"], right_new, local_sem.at[7]))
    stores[1].start()

    arrive(copies_c3)
    sums = total(s["c3"][...], s["d3"], range(1, 8))
    scale = jnp.sqrt(sums[0:1, 0:1] / (sums[0:1, 1:2] + graft_eps))
    arrive(copies_qz)
    arrive(copies_qy)
    for c in range(2):
        value = s["hy"][from_y[c]][4 * c : 4 * c + 4]
        update[:, c * B : c * B + 256] = value[:, 0:256] * scale
        update[:, c * B + 384 : (c + 1) * B] = value[:, 256:384] * scale
        update[:, c * B + 256 : c * B + 384] = s["hz"][from_z[c]][4 * c : 4 * c + 4] * scale

    for copy in started[early:]:
        copy.wait_send()
    for copy in stores:
        copy.wait()


def shards(acts, grads_out, owners, left_stats, right_stats, left_root, right_root):
    anywhere = pl.BlockSpec(memory_space=pl.ANY)
    stat = jax.ShapeDtypeStruct((B, B), BF16)
    update, left_new, right_new = pl.pallas_call(
        step_kernel,
        out_shape=(jax.ShapeDtypeStruct((4, 1024), F32), stat, stat),
        in_specs=[anywhere] * 7,
        out_specs=(pl.BlockSpec(memory_space=pltpu.VMEM), anywhere, anywhere),
        scratch_shapes=[pltpu.VMEM(shape, dtype) for shape, dtype in SCRATCH.values()]
        + [
            pltpu.SemaphoreType.DMA((EXCHANGES,)),
            pltpu.SemaphoreType.DMA((EXCHANGES,)),
            pltpu.SemaphoreType.DMA((9,)),
            pltpu.SMEM((2, 4), jnp.int32),
        ],
        compiler_params=pltpu.CompilerParams(collective_id=0, has_side_effects=True, vmem_limit_bytes=int(52.5 * 2**20)),
        name="shampoo_step",
    )(owners, acts, grads_out, left_stats[0, 0], right_stats[0, 0], left_root[0, 0], right_root[0, 0])
    return (update.astype(BF16), left_new.reshape(left_stats.shape), right_new.reshape(right_stats.shape))


def solution(mesh):
    return jax.shard_map(
        shards,
        mesh=mesh,
        in_specs=(
            P("dp", None),
            P("dp", "mp"),
            P(),
            P("dp", "mp", None, None),
            P("dp", "mp", None, None),
            P("dp", "mp", None, None),
            P("dp", "mp", None, None),
        ),
        out_specs=(P("dp", "mp"), P("dp", "mp", None, None), P("dp", "mp", None, None)),
        check_vma=False,
    )
```

```python
import functools

import jax
import jax.numpy as jnp
from jax import lax
from jax.experimental import pallas as pl
from jax.experimental.pallas import tpu as pltpu
from jax.sharding import PartitionSpec as P

stat_decay = 0.9
graft_eps = 1e-06
MESH = pl.DeviceIdType.MESH
SIZE = {"y": 8, "z": 8, "x": 4}
SEND_ORDER = {8: (4, 3, 5, 2, 6, 1, 7), 4: (2, 1, 3)}
B = 512
F32 = jnp.float32
BF16 = jnp.bfloat16

SCRATCH = dict(
    a=((256, 1024), BF16),
    at=((1024, 256), BF16),
    g=((256, 1024), BF16),
    left_old=((B, B), BF16),
    right_old=((B, B), BF16),
    left_root=((B, B), BF16),
    right_root=((B, B), BF16),
    sy=((8, 4, 64, 128), BF16),
    sz=((8, 4, 64, 128), BF16),
    sx=((4, 2, 4, 128, 128), BF16),
    fy=((2, 4, 64, 128), BF16),
    fz=((2, 4, 64, 128), BF16),
    fx=((2, 4, 128, 128), BF16),
    ey=((2, 2, 64, 128), BF16),
    ez=((2, 2, 64, 128), BF16),
    qy1=((2, 4, 64, 128), BF16),
    qz1=((2, 4, 64, 128), BF16),
    qx1=((2, 4, 128, 128), BF16),
    ry=((4, 4, 64, 128), BF16),
    rz=((4, 4, 64, 128), BF16),
    rx=((2, 2, 4, 128, 128), BF16),
    m2z=((8, 96, 128), BF16),
    m2y=((8, 96, 128), BF16),
    r2z=((8, 96, 128), BF16),
    r2y=((8, 96, 128), BF16),
    m3x=((64, 128), BF16),
    m3y=((64, 128), BF16),
    m3z=((64, 128), BF16),
    r3x=((4, 64, 128), BF16),
    r3y=((8, 64, 128), BF16),
    r3z=((8, 64, 128), BF16),
    g4z=((8, 96, 128), BF16),
    g4y=((8, 96, 128), BF16),
    m5y=((8, 64, 128), BF16),
    m5z=((8, 64, 128), BF16),
    m5x=((4, 2, 128, 128), BF16),
    g5y=((8, 64, 128), BF16),
    g5z=((8, 64, 128), BF16),
    g5x=((4, 2, 128, 128), BF16),
    block=((B, B), BF16),
    perm1=((B, B), BF16),
    perm2=((B, B), BF16),
    left1=((B, B), BF16),
    left2=((B, B), BF16),
    ta=((8, 4, 16, 256), BF16),
    tbc=((4, 2, 128, 128), BF16),
    ua=((8, 4, 16, 256), BF16),
    ubc=((4, 2, 128, 128), BF16),
    va=((4, 4, 16, 256), BF16),
    vb=((8, 2, 32, 128), BF16),
    vc=((8, 4, 16, 128), BF16),
    wa=((4, 4, 16, 256), BF16),
    wb=((8, 2, 32, 128), BF16),
    wc=((8, 4, 16, 128), BF16),
    qy=((8, 8, 384), F32),
    qz=((8, 8, 128), F32),
    hy=((8, 8, 384), F32),
    hz=((8, 8, 128), F32),
    c0=((8, 128), F32),
    c1=((8, 128), F32),
    c2=((8, 128), F32),
    c3=((8, 128), F32),
    d0=((8, 128), F32),
    d1=((4, 8, 128), F32),
    d2=((8, 8, 128), F32),
    d3=((8, 8, 128), F32),
    left_out=((B, B), BF16),
    right_out=((B, B), BF16),
)
EXCHANGES = 46


def dot(lhs, rhs, contract=((1,), (0,))):
    return lax.dot_general(lhs, rhs, (contract, ((), ())), preferred_element_type=F32)


def step_kernel(owners_in, acts, grads, left_stats, right_stats, left_roots, right_roots, update, left_new, right_new, *rest):
    s = dict(zip(SCRATCH, rest))
    send_sem, recv_sem, local_sem = rest[len(SCRATCH) : len(SCRATCH) + 3]
    me = lax.axis_index("dp")
    core = lax.axis_index("mp")
    at = {"y": me // 32, "z": (me // 4) % 8, "x": me % 4}
    my_y, my_z, my_x = at["y"], at["z"], at["x"]

    def index_of(y, z, x):
        return (y * 8 + z) * 4 + x

    def partner(axis, d):
        there = dict(at)
        there[axis] = (at[axis] + d) % SIZE[axis]
        return there[axis], index_of(**there)

    loads = []
    for k, (src, name) in enumerate(
        ((acts, "a"), (grads, "g"), (left_roots, "left_root"), (right_roots, "right_root"), (left_stats, "left_old"), (right_stats, "right_old"))
    ):
        loads.append(pltpu.make_async_copy(src, s[name], local_sem.at[k]))
    for k, (src, name) in enumerate(((acts, "a"), (grads, "g"))):
        for part in range(4):
            rows = pl.ds(part * 64, 64)
            pltpu.make_async_copy(src.at[rows], s[name].at[rows], local_sem.at[k]).start()

    owners = rest[len(SCRATCH) + 3]
    load_owners = pltpu.make_async_copy(owners_in, owners, local_sem.at[8])
    load_owners.start()

    barrier = pltpu.get_barrier_semaphore()
    greeted = 0
    for axis in ("y", "z", "x"):
        for d in SEND_ORDER[SIZE[axis]]:
            pl.semaphore_signal(barrier, inc=1, device_id=(partner(axis, d)[1], core), device_id_type=MESH)
            greeted += 1
    pl.semaphore_signal(barrier, inc=1, device_id=(me, 1 - core), device_id_type=MESH)
    greeted += 1

    used = [0]
    started = []

    def remote(src, dst, k, dp, mp):
        return pltpu.make_async_remote_copy(
            src_ref=src, dst_ref=dst, send_sem=send_sem.at[k], recv_sem=recv_sem.at[k], device_id=(dp, mp), device_id_type=MESH
        )

    def exchange(axis, src, into, dst=None):
        k = used[0]
        used[0] += 1
        n = SIZE[axis]
        for d in SEND_ORDER[n]:
            t, dp = partner(axis, d)
            remote(src(t, d), dst(d) if dst else s[into].at[d], k, dp, core).start()
        slots = s[into].at[0 : n - 1]
        started.append(remote(slots, slots, k, partner(axis, 1)[1], core))
        return started[-1]

    def send(src, dst, dp, mp):
        k = used[0]
        used[0] += 1
        copy = remote(src, dst, k, dp, mp)
        copy.start()
        started.append(copy)
        return copy

    def arrive(*copies):
        for copy in copies:
            copy.wait_recv()

    def total(own, received, n, *index):
        value = own.astype(F32)
        for d in n:
            value = value + received[(d, *index)].astype(F32)
        return value

    loads[0].wait()
    loads[1].wait()
    for k in range(4):
        s["at"][k * 256 : (k + 1) * 256] = s["a"][:, k * 256 : (k + 1) * 256].T

    def products(lane):
        for r in range(2):
            for c in range(2):
                rhs = s["g"][:, c * B + lane : c * B + lane + 256]
                yield 2 * r + c, dot(s["at"][r * B : (r + 1) * B], rhs).astype(BF16)

    for b, value in products(0):
        for t in range(8):
            s["sy"][t, b] = value[t * 64 : (t + 1) * 64, :128]
            s["sz"][t, b] = value[t * 64 : (t + 1) * 64, 128:]
    pl.semaphore_wait(barrier, greeted)
    def away(axis, d):
        t, dp = partner(axis, d % SIZE[axis])
        return t, dp

    def first_sends(axis, own, full, half):
        t4 = away(axis, 4)[0]
        h0 = send(s[own].at[t4, 0:2], s[half].at[0], away(axis, 2)[1], core)
        h1 = send(s[own].at[t4, 2:4], s[half].at[1], away(axis, -2)[1], core)
        f0 = send(s[own].at[away(axis, 3)[0]], s[full].at[0], away(axis, 1)[1], core)
        f1 = send(s[own].at[away(axis, -3)[0]], s[full].at[1], away(axis, -1)[1], core)
        return [f0, f1, h0, h1]

    def neighbour_sends(axis, own, received):
        return [send(s[own].at[away(axis, d)[0]], s[received].at[k], away(axis, d)[1], core) for k, d in enumerate((1, -1))]

    relay_y = first_sends("y", "sy", "fy", "ey")
    relay_z = first_sends("z", "sz", "fz", "ez")
    copies_y = neighbour_sends("y", "sy", "ry")
    copies_z = neighbour_sends("z", "sz", "rz")

    for b, value in products(256):
        for t in range(4):
            s["sx"][t, 0, b] = value[t * 128 : (t + 1) * 128, :128]
            s["sx"][t, 1, b] = value[t * 128 : (t + 1) * 128, 128:]
    relay_x = [send(s["sx"].at[away("x", 2)[0], k], s["fx"].at[k], away("x", d)[1], core) for k, d in enumerate((1, -1))]
    copies_x = [send(s["sx"].at[away("x", d)[0], 1 - k], s["rx"].at[k, 1 - k], away("x", d)[1], core) for k, d in enumerate((1, -1))]

    for load in loads[2:]:
        load.start()

    def merge(axis, own, full, half, merged, received):
        copies = []
        for k, d in enumerate((2, -2)):
            t, dp = away(axis, d)
            for b in range(4):
                value = s[own][t, b].astype(F32) + s[full][k, b].astype(F32)
                if b // 2 == k:
                    value = value + s[half][k, b % 2].astype(F32)
                s[merged][k, b] = value.astype(BF16)
            copies.append(send(s[merged].at[k], s[received].at[2 + k], dp, core))
        return copies

    arrive(*relay_y)
    copies_y += merge("y", "sy", "fy", "ey", "qy1", "ry")
    arrive(*relay_z)
    copies_z += merge("z", "sz", "fz", "ez", "qz1", "rz")
    arrive(*relay_x)
    for k, d in enumerate((1, -1)):
        t, dp = away("x", d)
        for b in range(4):
            s["qx1"][k, b] = (s["sx"][t, k, b].astype(F32) + s["fx"][k, b].astype(F32)).astype(BF16)
        copies_x.append(send(s["qx1"].at[k], s["rx"].at[k, k], dp, core))

    arrive(*copies_x)
    for t in range(8):
        b, half = t // 2, (t % 2) * 64
        for which, name in ((0, "m2y"), (1, "m2z")):
            index = (which, b, slice(half, half + 64))
            s[name][t, 32:96] = total(s["sx"][(my_x, *index)], s["rx"], range(2), *index).astype(BF16)

    def narrow_sums(own, received, name, place):
        for t in range(8):
            index = (t // 2, slice((t % 2) * 32, (t % 2) * 32 + 32))
            s[name][t, 0:32] = total(own[(place, *index)], received, range(4), *index).astype(BF16)

    arrive(*copies_y)
    narrow_sums(s["sy"], s["ry"], "m2z", my_y)
    copies_z2 = exchange("z", lambda t, d: s["m2z"].at[t], "r2z")
    arrive(*copies_z)
    narrow_sums(s["sz"], s["rz"], "m2y", my_z)
    copies_y2 = exchange("y", lambda t, d: s["m2y"].at[t], "r2y")

    row = lax.broadcasted_iota(jnp.int32, (B, B), 0)
    col = lax.broadcasted_iota(jnp.int32, (B, B), 1)
    x_part, k_part = row // 128, row % 4
    source1 = ((row // 4) % 4) * 128 + ((row // 16) % 8) * 16 + x_part * 4 + k_part
    source2 = ((row // 32) % 4) * 128 + ((row // 4) % 8) * 16 + x_part * 4 + k_part
    loads[2].wait()
    for source, name in ((source1, "perm1"), (source2, "perm2")):
        pick = jnp.where(col == source, 1.0, 0.0).astype(BF16)
        s[name][...] = dot(pick, s["left_root"][...]).astype(BF16)

    arrive(copies_z2)
    value = total(s["m2z"][my_z], s["r2z"], range(1, 8)).astype(BF16)
    s["m3x"][0:32] = value[:32]
    s["m3y"][...] = value[32:]
    copies_y3 = exchange("y", lambda t, d: s["m3y"], "r3y")
    arrive(copies_y2)
    value = total(s["m2y"][my_y], s["r2y"], range(1, 8)).astype(BF16)
    s["m3x"][32:64] = value[:32]
    s["m3z"][...] = value[32:]
    copies_z3 = exchange("z", lambda t, d: s["m3z"], "r3z")
    copies_x3 = exchange("x", lambda t, d: s["m3x"], "r3x")

    arrive(copies_x3)
    value = total(s["m3x"][...], s["r3x"], range(1, 4)).astype(BF16)
    s["g4z"][my_z, 0:32] = value[:32]
    s["g4y"][my_y, 0:32] = value[32:]
    arrive(copies_y3)
    s["g4z"][my_z, 32:96] = total(s["m3y"][...], s["r3y"], range(1, 8)).astype(BF16)
    copies_z4 = exchange("z", lambda t, d: s["g4z"].at[my_z], "g4z", lambda d: s["g4z"].at[my_z])
    arrive(copies_z3)
    s["g4y"][my_y, 32:96] = total(s["m3z"][...], s["r3z"], range(1, 8)).astype(BF16)
    copies_y4 = exchange("y", lambda t, d: s["g4y"].at[my_y], "g4y", lambda d: s["g4y"].at[my_y])

    load_owners.wait()
    owner = [owners[core, b] for b in range(4)]
    owner_y = [o // 32 for o in owner]
    owner_z = [(o // 4) % 8 for o in owner]
    owner_x = [o % 4 for o in owner]

    def block_of(dp):
        b = jnp.int32(0)
        for k in range(1, 4):
            b = jnp.where(owner[k] == dp, k, b)
        return b

    my_block = block_of(me)
    is_owner = (owner[0] == me) | (my_block > 0)

    arrive(copies_z4)

    def narrow_part(source, b):
        return jnp.concatenate([s[source][2 * b, 0:32], s[source][2 * b + 1, 0:32]], axis=0)

    def wide_part(source, b):
        return jnp.concatenate([s[source][2 * b, 32:96], s[source][2 * b + 1, 32:96]], axis=0)

    for d in range(1, 8):
        s["m5y"][d] = narrow_part("g4z", block_of(partner("y", d)[1]))
    copies_y5 = exchange("y", lambda t, d: s["m5y"].at[d], "g5y", lambda d: s["g5y"].at[my_y])
    s["g5y"][my_y] = narrow_part("g4z", my_block)
    for d in range(1, 4):
        s["m5x"][d, 1] = wide_part("g4z", block_of(partner("x", d)[1]))
    s["g5x"][my_x, 1] = wide_part("g4z", my_block)
    arrive(copies_y4)
    for d in range(1, 4):
        s["m5x"][d, 0] = wide_part("g4y", block_of(partner("x", d)[1]))
    copies_x5 = exchange("x", lambda t, d: s["m5x"].at[d], "g5x", lambda d: s["g5x"].at[my_x])
    for d in range(1, 8):
        s["m5z"][d] = narrow_part("g4y", block_of(partner("z", d)[1]))
    copies_z5 = exchange("z", lambda t, d: s["m5z"].at[d], "g5z", lambda d: s["g5z"].at[my_z])
    s["g5x"][my_x, 0] = wide_part("g4y", my_block)
    s["g5z"][my_z] = narrow_part("g4y", my_block)

    def left_product(name, into, lo, hi):
        s[into][:, lo:hi] = dot(s[name][...], s["block"][:, lo:hi]).astype(BF16)

    loads[3].wait()
    arrive(copies_y5)
    for k in range(8):
        s["block"][k * 64 : (k + 1) * 64, 0:128] = s["g5y"][k]
    arrive(copies_x5)
    for k in range(4):
        s["block"][k * 128 : (k + 1) * 128, 256:384] = s["g5x"][k, 0]
        s["block"][k * 128 : (k + 1) * 128, 384:512] = s["g5x"][k, 1]
    left_product("perm1", "left1", 256, 512)
    left_product("perm2", "left2", 256, 512)
    arrive(copies_z5)
    for k in range(8):
        s["block"][k * 64 : (k + 1) * 64, 128:256] = s["g5z"][k]
    left_product("perm1", "left1", 0, 256)
    left_product("perm2", "left2", 0, 256)
    one_block = s["block"][...]
    left1 = s["left1"][...]
    part_a = dot(left1, s["right_root"][:, 0:256]).astype(BF16)
    for k in range(4):
        for z in range(8):
            row0 = (k * 8 + z) * 16
            s["ta"][z, k] = part_a[row0 : row0 + 16]
    copies_ta = exchange("z", lambda t, d: s["ta"].at[t], "ua", lambda d: s["ua"].at[my_z])
    s["ua"][my_z] = s["ta"][my_z]
    left2 = s["left2"][...]
    part_b = dot(left2, s["right_root"][:, 256:384]).astype(BF16)
    part_c = dot(left1, s["right_root"][:, 384:512]).astype(BF16)
    for k in range(4):
        s["tbc"][k, 0] = part_b[k * 128 : (k + 1) * 128]
        s["tbc"][k, 1] = part_c[k * 128 : (k + 1) * 128]
    copies_tbc = exchange("x", lambda t, d: s["tbc"].at[t], "ubc", lambda d: s["ubc"].at[my_x])
    s["ubc"][my_x] = s["tbc"][my_x]

    def square_sum(value):
        value = value.astype(F32)
        return jnp.sum(jnp.sum(value * value, axis=0, keepdims=True), axis=1, keepdims=True)

    grad_square = square_sum(one_block)
    precond_square = square_sum(part_a) + square_sum(part_b) + square_sum(part_c)
    lane = lax.broadcasted_iota(jnp.int32, (8, 128), 1)
    both = jnp.where(lane == 0, grad_square, precond_square)
    s["c0"][...] = jnp.where(is_owner, both, jnp.zeros_like(both))
    copy_c0 = send(s["c0"], s["d0"], me, 1 - core)

    def new_stat(old, gram):
        old = old.astype(F32)
        return jnp.where(is_owner, stat_decay * old + (1.0 - stat_decay) * gram / B, old).astype(BF16)

    arrive(copy_c0)
    s["c1"][...] = s["c0"][...] + s["d0"][...]
    copies_c1 = exchange("x", lambda t, d: s["c1"], "d1")

    early = len(started) - 4
    for copy in started[:early]:
        copy.wait_send()

    arrive(copies_tbc)
    arrive(copies_c1)
    s["c2"][...] = total(s["c1"][...], s["d1"], range(1, 4))
    copies_c2 = exchange("y", lambda t, d: s["c2"], "d2")
    for t in range(8):
        for c in range(2):
            b = 2 * (t // 4) + c
            s["vb"][t, c] = s["ubc"][owner_x[b], 0, (t % 4) * 32 : (t % 4) * 32 + 32]
        for b in range(4):
            s["vc"][t, b] = s["ubc"][owner_x[b], 1, t * 16 : (t + 1) * 16]
    copies_vb = exchange("y", lambda t, d: s["vb"].at[t], "wb", lambda d: s["wb"].at[my_y])
    copies_vc = exchange("z", lambda t, d: s["vc"].at[t], "wc", lambda d: s["wc"].at[my_z])
    s["wb"][my_y] = s["vb"][my_y]
    s["wc"][my_z] = s["vc"][my_z]
    arrive(copies_ta)
    for t in range(4):
        for b in range(4):
            s["va"][t, b] = s["ua"][owner_z[b], t]
    copies_va = exchange("x", lambda t, d: s["va"].at[t], "wa", lambda d: s["wa"].at[my_x])
    s["wa"][my_x] = s["va"][my_x]
    arrive(copies_c2)
    s["c3"][...] = total(s["c2"][...], s["d2"], range(1, 8))
    copies_c3 = exchange("z", lambda t, d: s["c3"], "d3")

    loads[4].wait()
    s["left_out"][...] = new_stat(s["left_old"][...], dot(one_block, one_block, ((1,), (1,))))
    stores = [pltpu.make_async_copy(s["left_out"], left_new, local_sem.at[6])]
    stores[0].start()

    my_half = my_y // 4
    arrive(copies_vb)
    from_y, from_z = [], []
    for c in range(2):
        o = owners[core, 2 * my_half + c]
        from_y.append(o // 32)
        from_z.append((o // 4) % 8)
    for c in range(2):
        value = s["wb"][from_y[c], c].astype(F32)
        for t in range(8):
            s["qz"][t, 4 * c : 4 * c + 4] = value[4 * t : 4 * t + 4]
    copies_qz = exchange("z", lambda t, d: s["qz"].at[t], "hz", lambda d: s["hz"].at[my_z])
    s["hz"][my_z] = s["qz"][my_z]
    arrive(copies_vc)
    arrive(copies_va)
    for b in range(4):
        r, c = b // 2, b % 2
        value_a = s["wa"][owner_x[b], b].astype(F32)
        value_c = s["wc"][owner_z[b], b].astype(F32)
        for k in range(4):
            s["qy"][4 * r + k, 4 * c : 4 * c + 4, 0:256] = value_a[4 * k : 4 * k + 4]
            s["qy"][4 * r + k, 4 * c : 4 * c + 4, 256:384] = value_c[4 * k : 4 * k + 4]
    copies_qy = exchange("y", lambda t, d: s["qy"].at[t], "hy", lambda d: s["hy"].at[my_y])
    s["hy"][my_y] = s["qy"][my_y]

    loads[5].wait()
    s["right_out"][...] = new_stat(s["right_old"][...], dot(one_block, one_block, ((0,), (0,))))
    stores.append(pltpu.make_async_copy(s["right_out"], right_new, local_sem.at[7]))
    stores[1].start()

    arrive(copies_c3)
    sums = total(s["c3"][...], s["d3"], range(1, 8))
    scale = jnp.sqrt(sums[0:1, 0:1] / (sums[0:1, 1:2] + graft_eps))
    arrive(copies_qz)
    arrive(copies_qy)
    for c in range(2):
        value = s["hy"][from_y[c]][4 * c : 4 * c + 4]
        update[:, c * B : c * B + 256] = value[:, 0:256] * scale
        update[:, c * B + 384 : (c + 1) * B] = value[:, 256:384] * scale
        update[:, c * B + 256 : c * B + 384] = s["hz"][from_z[c]][4 * c : 4 * c + 4] * scale

    for copy in started[early:]:
        copy.wait_send()
    for copy in stores:
        copy.wait()


def shards(acts, grads_out, owners, left_stats, right_stats, left_root, right_root):
    anywhere = pl.BlockSpec(memory_space=pl.ANY)
    stat = jax.ShapeDtypeStruct((B, B), BF16)
    update, left_new, right_new = pl.pallas_call(
        step_kernel,
        out_shape=(jax.ShapeDtypeStruct((4, 1024), F32), stat, stat),
        in_specs=[anywhere] * 7,
        out_specs=(pl.BlockSpec(memory_space=pltpu.VMEM), anywhere, anywhere),
        scratch_shapes=[pltpu.VMEM(shape, dtype) for shape, dtype in SCRATCH.values()]
        + [
            pltpu.SemaphoreType.DMA((EXCHANGES,)),
            pltpu.SemaphoreType.DMA((EXCHANGES,)),
            pltpu.SemaphoreType.DMA((9,)),
            pltpu.SMEM((2, 4), jnp.int32),
        ],
        compiler_params=pltpu.CompilerParams(collective_id=0, has_side_effects=True, vmem_limit_bytes=int(52.5 * 2**20)),
        name="shampoo_step",
    )(owners, acts, grads_out, left_stats[0, 0], right_stats[0, 0], left_root[0, 0], right_root[0, 0])
    return (update.astype(BF16), left_new.reshape(left_stats.shape), right_new.reshape(right_stats.shape))


def solution(mesh):
    return jax.shard_map(
        shards,
        mesh=mesh,
        in_specs=(
            P("dp", None),
            P("dp", "mp"),
            P(),
            P("dp", "mp", None, None),
            P("dp", "mp", None, None),
            P("dp", "mp", None, None),
            P("dp", "mp", None, None),
        ),
        out_specs=(P("dp", "mp"), P("dp", "mp", None, None), P("dp", "mp", None, None)),
        check_vma=False,
    )
```
